512 devices in a mesh: outer: 16 (over y, x), inner: 32 (over z, core).
Axes of the slice: x: 4, y: 4, z: 16, core: 2. Of those that a mesh axis runs over, the one named last changes fastest.
Arguments:
- start_state: float32 [192, 512], replicated, may hold values from -6 to 6
- guess: float32 [512, 192, 512], P(('outer', 'inner')), may hold values from -6 to 6
- weight_in: bfloat16 [1024, 512, 1024], P(('outer', 'inner')), may hold values from -0.25 to 0.25
- weight_out: bfloat16 [1024, 1024, 512], P(('outer', 'inner')), may hold values from -0.1875 to 0.1875
- norm_gain: float32 [1024, 512], P(('outer', 'inner')), may hold values from 0.1 to 1.9
- coarse_gain: float32 [16, 512], P('outer'), may hold values from 0.6 to 1
Outputs:
- final_states: float32 [512, 192, 512], P(('outer', 'inner'))
The draws below stay inside these ranges and needn't reach their ends.
All inputs are finite; a program needn't handle non-finite values.
Results may differ from the reference program's by a relative error of at most 0.006.
Values sent between devices are 32-bit elements; how exact they have to be, the bound alone decides.
No kernel may reach another device: no remote copies, remote signals or barrier semaphores. Data moves between devices by JAX's collectives and lax.ppermute only.
A program may use at most 64 MiB of HBM per device.

```python
import math
import jax
import jax.numpy as jnp
from jax import lax

D = 512
FF = 1024
TOK = 192
LAYERS_DEV = 2
BLOCKS = 512
LAYERS = 1024
N_OUTER = 16
N_INNER = 32


def shard_levels(rng, extent, shards, smallest, top_value):
    level, own = 1.0, jax.random.fold_in(rng, 6)
    for dim, shards_of in shards:
        draws = jnp.exp(jax.random.uniform(jax.random.fold_in(own, dim), (shards_of,), jnp.float32, smallest / len(shards), top_value / len(shards)))
        level = level * jnp.repeat(draws, extent[dim] // shards_of).reshape([-1 if axis == dim else 1 for axis in range(len(extent))])
    return level


def bell_draw(rng, shape, deviation, most, shards=(), kind=jnp.bfloat16):
    drawn = jax.random.normal(rng, shape, jnp.float32) * deviation
    if len(shards) > 0:
        drawn = shard_levels(rng, shape, shards, -0.22, 0.18) * drawn
    return jnp.clip(drawn, min=-most, max=most).astype(kind)


def setup_inputs(seed: int = 0) -> dict:
    keys = jax.random.split(jax.random.key(seed), 7)
    return {
        "start_state": bell_draw(keys[0], (TOK, D), 1.0, 6.0, (), jnp.float32),
        "guess": bell_draw(keys[1], (BLOCKS, TOK, D), 1.0, 6.0, ((0, 512),), jnp.float32),
        "weight_in": bell_draw(keys[2], (LAYERS, D, FF), D ** -0.5, 0.25, ((0, 512),)),
        "weight_out": bell_draw(keys[3], (LAYERS, FF, D), FF ** -0.5, 0.1875, ((0, 512),)),
        "norm_gain": jnp.clip(1.0 + 0.18 * jax.random.normal(keys[4], (LAYERS, D), jnp.float32), 0.1, 1.9),
        "coarse_gain": jnp.clip(jnp.exp(math.log(1.0) - 0.5108256 * jax.random.uniform(keys[5], (N_OUTER, D), jnp.float32) ** shard_levels(keys[5], (N_OUTER, D), ((0, 16),), -0.2, 0.2)), 0.6, 1.0),
    }


step_size = 0.5

def layer(state, weight_in, weight_out, gain):
    meansq = lax.optimization_barrier(jnp.mean(state * state, axis=-1, keepdims=True))
    normed = (state * lax.rsqrt(meansq + 1e-06) * gain).astype(jnp.bfloat16)
    hidden = jax.nn.gelu(jnp.dot(normed, weight_in, preferred_element_type=jnp.float32)).astype(jnp.bfloat16)
    return state + step_size * jnp.dot(hidden, weight_out, preferred_element_type=jnp.float32)

def run_block(state, weight_in, weight_out, gain):
    for level in range(LAYERS_DEV):
        state = layer(state, weight_in[level], weight_out[level], gain[level])
    return state

def sweep(states, start_state, weight_in, weight_out, norm_gain):
    inputs = jnp.concatenate([start_state[None], states[:-1]], axis=0)
    win = weight_in.reshape(BLOCKS, LAYERS_DEV, D, FF)
    wout = weight_out.reshape(BLOCKS, LAYERS_DEV, FF, D)
    gains = norm_gain.reshape(BLOCKS, LAYERS_DEV, D)
    return lax.map(lambda item: run_block(*item), (inputs, win, wout, gains))

def reference(start_state, guess, weight_in, weight_out, norm_gain, coarse_gain):
    first = sweep(guess, start_state, weight_in, weight_out, norm_gain)
    second = sweep(first, start_state, weight_in, weight_out, norm_gain)
    third = sweep(second, start_state, weight_in, weight_out, norm_gain)
    defect = third - second
    group_defect = lax.optimization_barrier(jnp.sum(defect.reshape(N_OUTER, N_INNER, TOK, D), axis=1)) / N_INNER

    def advance(carry, item):
        gain, term = item
        updated = gain[None] * carry + term
        return (updated, (carry, updated))
    start = jnp.zeros((TOK, D), dtype=jnp.float32)
    unused, (earlier, current) = lax.scan(advance, start, (coarse_gain, group_defect))
    weights = ((jnp.arange(N_INNER) + 1).astype(jnp.float32) / N_INNER).reshape(1, N_INNER, 1, 1)
    corrected = third.reshape(N_OUTER, N_INNER, TOK, D) + weights * current[:, None] + (1.0 - weights) * earlier[:, None]
    corrected = corrected.reshape(BLOCKS, TOK, D)
    return sweep(corrected, start_state, weight_in, weight_out, norm_gain)
```

```python
import jax
import jax.numpy as jnp
from jax import lax
from jax.sharding import Mesh, PartitionSpec as P

step_size = 0.5
ALL = ("outer", "z", "core")


def from_odd(value):
    peers = lax.axis_size(ALL)
    return lax.ppermute(value, ALL, [(i, i + 1) for i in range(1, peers - 1, 2)])


def from_pair(value):
    return lax.all_gather(value, "core", axis=0)


def to_each(value, axis):
    peers = lax.axis_size(axis)
    copies = jnp.broadcast_to(value[None], (peers,) + value.shape)
    return lax.all_to_all(copies, axis, 0, 0, tiled=True)


def layer(state, weight_in, weight_out, gain):
    meansq = jnp.mean(state * state, axis=-1, keepdims=True)
    normed = (state * lax.rsqrt(meansq + 1e-06) * gain).astype(jnp.bfloat16)
    hidden = jax.nn.gelu(jnp.dot(normed, weight_in, preferred_element_type=jnp.float32)).astype(
        jnp.bfloat16
    )
    return state + step_size * jnp.dot(hidden, weight_out, preferred_element_type=jnp.float32)


def coarse(gain, part):
    places = lax.axis_size("z")
    groups = lax.axis_size("outer")
    count = places * lax.axis_size("core")
    rows = part.shape[0] // places
    blocks = part.reshape(places, rows, part.shape[1])
    own = jnp.sum(lax.all_to_all(blocks, "z", 0, 0, tiled=True), axis=0) / count
    heard = to_each(jnp.concatenate([own, gain], axis=0), "outer")
    group = lax.axis_index("outer")
    running = jnp.zeros_like(own)
    earlier = jnp.zeros_like(own)
    for index in range(groups):
        earlier = jnp.where(index == group, running, earlier)
        running = heard[index, rows:] * running + heard[index, :rows]
    current = gain * earlier + own
    both = jnp.concatenate([earlier, current], axis=1)
    both = lax.all_gather(both, "z", axis=0, tiled=True)
    both = lax.all_gather(both, "core", axis=0, tiled=True)
    return jnp.split(both, 2, axis=1)


def per_device(start_state, guess, weight_in, weight_out, norm_gain, coarse_gain):
    core = lax.axis_index("core")
    is_first = lax.axis_index(ALL) == 0
    is_odd = core == 1
    tokens = start_state.shape[0]

    def block(state):
        for level in range(weight_in.shape[0]):
            state = layer(state, weight_in[level], weight_out[level], norm_gain[level])
        return state

    def arrived(value):
        return jnp.where(is_first, start_state, value)

    guess_z = from_odd(guess[0])
    guess_pair = from_pair(guess[0])
    first = block(jnp.where(is_odd, guess_pair[0], arrived(guess_z)))
    first_z = from_odd(first)
    first_pair = from_pair(first)
    second_odd = block(first_pair[0])
    second_z = from_odd(second_odd)
    second_even = block(arrived(first_z))
    second_pair = from_pair(jnp.where(is_odd, second_odd, second_even))
    third = block(jnp.where(is_odd, second_pair[0], arrived(second_z)))
    third_pair = from_pair(third)
    third_z = from_odd(third)

    half = tokens // 2

    def mine(value):
        return lax.dynamic_slice_in_dim(value, core * half, half, 1)

    defects = mine(third_pair) - mine(second_pair)
    earlier, current = coarse(coarse_gain, defects[0] + defects[1])
    count = lax.axis_size("z") * lax.axis_size("core")
    weight = lax.axis_index(("z", "core")).astype(jnp.float32) / count
    moved = jnp.where(is_odd, third_pair[0], third_z)
    corrected = moved + weight * current + (1.0 - weight) * earlier
    return block(arrived(corrected))[None]


def solution(mesh):
    groups, inner = mesh.devices.shape
    fine = Mesh(mesh.devices.reshape(groups, inner // 2, 2), ALL)
    split = P(ALL, None, None)
    return jax.shard_map(
        per_device,
        mesh=fine,
        in_specs=(P(), split, split, split, P(ALL, None), P("outer", None)),
        out_specs=split,
        check_vma=False,
    )
```

```python
import functools

import jax
import jax.numpy as jnp
from jax import lax
from jax.experimental import pallas as pl
from jax.experimental.pallas import tpu as pltpu
from jax.sharding import Mesh, PartitionSpec as P

step_size = 0.5
ALL = ("outer", "z", "core")
LANES = 128


def from_odd(value):
    peers = lax.axis_size(ALL)
    return lax.ppermute(value, ALL, [(i, i + 1) for i in range(1, peers - 1, 2)])


def from_pair(value):
    return lax.all_gather(value, "core", axis=0)


def gelu(value):
    root = 0.7978845608028654
    inner = value * (root + (root * 0.044715) * (value * value))
    half = 0.5 * value
    return half + half * jnp.tanh(inner)


def layers(state, weight_in, weight_out, norm_gain):
    for level in range(weight_in.shape[0]):
        meansq = jnp.mean(state * state, axis=-1, keepdims=True)
        normed = (state * lax.rsqrt(meansq + 1e-06) * norm_gain[level : level + 1, :]).astype(
            jnp.bfloat16
        )
        hidden = jnp.dot(normed, weight_in[level], preferred_element_type=jnp.float32)
        hidden = gelu(hidden).astype(jnp.bfloat16)
        state = state + step_size * jnp.dot(
            hidden, weight_out[level], preferred_element_type=jnp.float32
        )
    return state


def call(body, out_shape, args, name, flops=0):
    return pl.pallas_call(
        body,
        out_shape=jax.ShapeDtypeStruct(out_shape, jnp.float32),
        in_specs=[pl.BlockSpec(memory_space=pltpu.VMEM)] * len(args),
        out_specs=pl.BlockSpec(memory_space=pltpu.VMEM),
        compiler_params=pltpu.CompilerParams(vmem_limit_bytes=16 << 20),
        cost_estimate=pl.CostEstimate(
            flops=flops, bytes_accessed=sum(a.size * 4 for a in args), transcendentals=0
        ),
        name=name,
    )(*args)


def load_kernel(*refs):
    count = len(refs) // 3
    copies = [
        pltpu.make_async_copy(refs[at], refs[count + at], refs[2 * count + at])
        for at in range(count)
    ]
    for copy in copies:
        copy.start()
    for copy in copies:
        copy.wait()


def loaded(args):
    return pl.pallas_call(
        load_kernel,
        out_shape=[jax.ShapeDtypeStruct(a.shape, a.dtype) for a in args],
        in_specs=[pl.BlockSpec(memory_space=pl.ANY)] * len(args),
        out_specs=[pl.BlockSpec(memory_space=pltpu.VMEM)] * len(args),
        scratch_shapes=[pltpu.SemaphoreType.DMA(())] * len(args),
        compiler_params=pltpu.CompilerParams(vmem_limit_bytes=16 << 20),
        cost_estimate=pl.CostEstimate(
            flops=0,
            bytes_accessed=sum(a.size * a.dtype.itemsize for a in args),
            transcendentals=0,
        ),
        name="load",
    )(*args)


def is_odd():
    return lax.axis_index("core") == 1


def is_first():
    return lax.axis_index(ALL) == 0


def choose_kernel(pair, hop, start, weight_in, weight_out, norm_gain, out):
    even = jnp.where(is_first(), start[...], hop[...])
    state = jnp.where(is_odd(), pair[0], even)
    out[...] = layers(state, weight_in, weight_out, norm_gain)


def odd_kernel(pair, weight_in, weight_out, norm_gain, out):
    out[...] = layers(pair[0], weight_in, weight_out, norm_gain)


def even_kernel(ready, hop, start, weight_in, weight_out, norm_gain, out):
    even = jnp.where(is_first(), start[...], hop[...])
    state = layers(even, weight_in, weight_out, norm_gain)
    out[...] = jnp.where(is_odd(), ready[...], state)


def part_kernel(third, second, out):
    places, rows, lanes = out.shape
    tokens, width = third.shape[1:]
    half = width // 2
    across = half // lanes

    def piece(ref, which, at, right):
        down = pl.ds(at // across * rows, rows)
        side = pl.ds(right * half + at % across * lanes, lanes)
        return ref[which, down, side]

    for at in range(places):
        sums = []
        for right in range(2):
            sums.append(
                (piece(third, 0, at, right) - piece(second, 0, at, right))
                + (piece(third, 1, at, right) - piece(second, 1, at, right))
            )
        out[at] = jnp.where(is_odd(), sums[1], sums[0])


def gain_piece(gain, lanes):
    pieces = gain.shape[1] // lanes
    across = pieces // 2
    place = lax.axis_index("core") * across + lax.rem(lax.axis_index("z"), across)
    value = gain[:, 0:lanes]
    for at in range(1, pieces):
        value = jnp.where(place == at, gain[:, at * lanes : (at + 1) * lanes], value)
    return value


def own_kernel(count, parts, gain, out):
    places, rows, lanes = parts.shape
    own = parts[0]
    for at in range(1, places):
        own = own + parts[at]
    own = own / count
    spare = out.shape[1] - rows
    tail = jnp.broadcast_to(gain_piece(gain, lanes), (spare, lanes))
    for group in range(out.shape[0]):
        out[group, 0:rows, :] = own
        out[group, rows:, :] = tail


def scan_kernel(heard, out):
    groups = heard.shape[0]
    rows, lanes = out.shape[1:]
    group = lax.axis_index("outer")
    running = jnp.zeros((rows, lanes), jnp.float32)
    earlier, current = running, running
    for index in range(groups):
        earlier = jnp.where(index == group, running, earlier)
        running = heard[index, rows : rows + 1, :] * running + heard[index, 0:rows, :]
        current = jnp.where(index == group, running, current)
    out[0] = earlier
    out[1] = current


def last_kernel(both, pair, hop, start, weight_in, weight_out, norm_gain, out):
    cores, places, kinds, rows, lanes = both.shape
    count = places * cores
    place = lax.axis_index("z") * cores + lax.axis_index("core")
    weight = place.astype(jnp.float32) / count
    across = hop.shape[1] // lanes // cores
    columns = []
    for core in range(cores):
        for side in range(across):
            pieces = []
            for down in range(places // across):
                at = down * across + side
                pieces.append(weight * both[core, at, 1] + (1.0 - weight) * both[core, at, 0])
            columns.append(jnp.concatenate(pieces, axis=0))
    moved = jnp.where(is_odd(), pair[0], hop[...])
    state = moved + jnp.concatenate(columns, axis=1)
    state = jnp.where(is_first(), start[...], state)
    out[0] = layers(state, weight_in, weight_out, norm_gain)


def per_device(start_state, guess, weight_in, weight_out, norm_gain, coarse_gain):
    tokens, width = start_state.shape
    places, groups = lax.axis_size("z"), lax.axis_size("outer")
    cores = lax.axis_size("core")
    *params, start_state, coarse_gain = loaded(
        (weight_in, weight_out, norm_gain, start_state, coarse_gain)
    )
    params = tuple(params)
    flops = 4 * tokens * weight_in.size

    def block(body, args, name):
        return call(body, (tokens, width), args + params, name, flops)

    guess_z = from_odd(guess[0])
    guess_pair = from_pair(guess[0])
    first = block(choose_kernel, (guess_pair, guess_z, start_state), "first")
    first_z = from_odd(first)
    first_pair = from_pair(first)
    second_odd = block(odd_kernel, (first_pair,), "second_odd")
    second_z = from_odd(second_odd)
    second = block(even_kernel, (second_odd, first_z, start_state), "second")
    second_pair = from_pair(second)
    third = block(choose_kernel, (second_pair, second_z, start_state), "third")
    third_pair = from_pair(third)
    third_z = from_odd(third)

    rows = tokens * width // LANES // places // cores
    part = call(part_kernel, (places, rows, LANES), (third_pair, second_pair), "part")
    parts = lax.all_to_all(part, "z", 0, 0, tiled=True)
    own = call(
        functools.partial(own_kernel, places * cores),
        (groups, rows + 8, LANES),
        (parts, coarse_gain),
        "own",
    )
    heard = lax.all_to_all(own, "outer", 0, 0, tiled=True)
    both = call(scan_kernel, (2, rows, LANES), (heard,), "scan")
    both = lax.all_gather(lax.all_gather(both, "z", axis=0), "core", axis=0)
    return call(
        last_kernel,
        (1, tokens, width),
        (both, third_pair, third_z, start_state) + params,
        "last",
        flops,
    )


def solution(mesh):
    groups, inner = mesh.devices.shape
    fine = Mesh(mesh.devices.reshape(groups, inner // 2, 2), ALL)
    split = P(ALL, None, None)
    return jax.shard_map(
        per_device,
        mesh=fine,
        in_specs=(P(), split, split, split, P(ALL, None), P("outer", None)),
        out_specs=split,
        check_vma=False,
    )
```

```python
import functools

import jax
import jax.numpy as jnp
from jax import lax
from jax.experimental import pallas as pl
from jax.experimental.pallas import tpu as pltpu
from jax.sharding import Mesh, PartitionSpec as P

step_size = 0.5
ALL = ("outer", "z", "core")
LANES = 128


def from_odd(value):
    peers = lax.axis_size(ALL)
    return lax.ppermute(value, ALL, [(i, i + 1) for i in range(1, peers - 1, 2)])


def from_pair(value):
    return lax.all_gather(value, "core", axis=0)


def gelu(value):
    root = 0.7978845608028654
    inner = value * (root + (root * 0.044715) * (value * value))
    half = 0.5 * value
    return half + half * jnp.tanh(inner)


def layers(state, weight_in, weight_out, norm_gain):
    for level in range(weight_in.shape[0]):
        meansq = jnp.mean(state * state, axis=-1, keepdims=True)
        normed = (state * lax.rsqrt(meansq + 1e-06) * norm_gain[level : level + 1, :]).astype(
            jnp.bfloat16
        )
        hidden = jnp.dot(normed, weight_in[level], preferred_element_type=jnp.float32)
        hidden = gelu(hidden).astype(jnp.bfloat16)
        state = state + step_size * jnp.dot(
            hidden, weight_out[level], preferred_element_type=jnp.float32
        )
    return state


def call(body, out_shape, args, name, flops=0, after=()):
    count = len(args)

    def with_after(*refs):
        body(*refs[:count], refs[-1])

    return pl.pallas_call(
        with_after,
        out_shape=jax.ShapeDtypeStruct(out_shape, jnp.float32),
        in_specs=[pl.BlockSpec(memory_space=pltpu.VMEM)] * count
        + [pl.BlockSpec(memory_space=pl.ANY)] * len(after),
        out_specs=pl.BlockSpec(memory_space=pltpu.VMEM),
        compiler_params=pltpu.CompilerParams(vmem_limit_bytes=16 << 20),
        cost_estimate=pl.CostEstimate(
            flops=flops, bytes_accessed=sum(a.size * 4 for a in args), transcendentals=0
        ),
        name=name,
    )(*args, *after)


def load_kernel(*refs):
    count = len(refs) // 3
    copies = [
        pltpu.make_async_copy(refs[at], refs[count + at], refs[2 * count + at])
        for at in range(count)
    ]
    for copy in copies:
        copy.start()
    for copy in copies:
        copy.wait()


def loaded(args):
    return pl.pallas_call(
        load_kernel,
        out_shape=[pltpu.VMEM(a.shape, a.dtype) for a in args],
        in_specs=[pl.BlockSpec(memory_space=pl.ANY)] * len(args),
        out_specs=[pl.BlockSpec(memory_space=pltpu.VMEM)] * len(args),
        scratch_shapes=[pltpu.SemaphoreType.DMA(())] * len(args),
        compiler_params=pltpu.CompilerParams(vmem_limit_bytes=16 << 20),
        cost_estimate=pl.CostEstimate(
            flops=0,
            bytes_accessed=sum(a.size * a.dtype.itemsize for a in args),
            transcendentals=0,
        ),
        name="load",
    )(*[pltpu.with_memory_space_constraint(a, pltpu.HBM) for a in args])


def is_odd():
    return lax.axis_index("core") == 1


def is_first():
    return lax.axis_index(ALL) == 0


def choose_kernel(pair, hop, start, weight_in, weight_out, norm_gain, out):
    even = jnp.where(is_first(), start[...], hop[...])
    state = jnp.where(is_odd(), pair[0], even)
    out[...] = layers(state, weight_in, weight_out, norm_gain)


def odd_kernel(pair, weight_in, weight_out, norm_gain, out):
    out[...] = layers(pair[0], weight_in, weight_out, norm_gain)


def even_kernel(ready, hop, start, weight_in, weight_out, norm_gain, out):
    even = jnp.where(is_first(), start[...], hop[...])
    state = layers(even, weight_in, weight_out, norm_gain)
    out[...] = jnp.where(is_odd(), ready[...], state)


def part_kernel(third, second, out):
    places, rows, lanes = out.shape
    tokens, width = third.shape[1:]
    half = width // 2
    across = half // lanes

    def piece(ref, which, at, right):
        down = pl.ds(at // across * rows, rows)
        side = pl.ds(right * half + at % across * lanes, lanes)
        return ref[which, down, side]

    for at in range(places):
        sums = []
        for right in range(2):
            sums.append(
                (piece(third, 0, at, right) - piece(second, 0, at, right))
                + (piece(third, 1, at, right) - piece(second, 1, at, right))
            )
        out[at] = jnp.where(is_odd(), sums[1], sums[0])


def gain_piece(gain, lanes):
    pieces = gain.shape[1] // lanes
    across = pieces // 2
    place = lax.axis_index("core") * across + lax.rem(lax.axis_index("z"), across)
    value = gain[:, 0:lanes]
    for at in range(1, pieces):
        value = jnp.where(place == at, gain[:, at * lanes : (at + 1) * lanes], value)
    return value


def own_kernel(count, parts, gain, out):
    places, rows, lanes = parts.shape
    own = parts[0]
    for at in range(1, places):
        own = own + parts[at]
    own = own / count
    spare = out.shape[1] - rows
    tail = jnp.broadcast_to(gain_piece(gain, lanes), (spare, lanes))
    for group in range(out.shape[0]):
        out[group, 0:rows, :] = own
        out[group, rows:, :] = tail


def scan_kernel(heard, out):
    groups = heard.shape[0]
    rows, lanes = out.shape[1] // 2, out.shape[2]
    group = lax.axis_index("outer")
    running = jnp.zeros((rows, lanes), jnp.float32)
    earlier, current = running, running
    for index in range(groups):
        earlier = jnp.where(index == group, running, earlier)
        running = heard[index, rows : rows + 1, :] * running + heard[index, 0:rows, :]
        current = jnp.where(index == group, running, current)
    for place in range(out.shape[0]):
        out[place, 0:rows, :] = earlier
        out[place, rows:, :] = current


def last_kernel(both, pair, hop, start, weight_in, weight_out, norm_gain, out):
    cores, places = both.shape[:2]
    rows, lanes = both.shape[2] // 2, both.shape[3]
    count = places * cores
    place = lax.axis_index("z") * cores + lax.axis_index("core")
    weight = place.astype(jnp.float32) / count
    across = hop.shape[1] // lanes // cores
    columns = []
    for core in range(cores):
        for side in range(across):
            pieces = []
            for down in range(places // across):
                at = down * across + side
                earlier, current = both[core, at, 0:rows, :], both[core, at, rows:, :]
                pieces.append(weight * current + (1.0 - weight) * earlier)
            columns.append(jnp.concatenate(pieces, axis=0))
    moved = jnp.where(is_odd(), pair[0], hop[...])
    state = moved + jnp.concatenate(columns, axis=1)
    state = jnp.where(is_first(), start[...], state)
    out[0] = layers(state, weight_in, weight_out, norm_gain)


def per_device(start_state, guess, weight_in, weight_out, norm_gain, coarse_gain):
    tokens, width = start_state.shape
    places, groups = lax.axis_size("z"), lax.axis_size("outer")
    cores = lax.axis_size("core")
    *params, start_state, coarse_gain = loaded(
        (weight_in, weight_out, norm_gain, start_state, coarse_gain)
    )
    params = tuple(params)
    flops = 4 * tokens * weight_in.size

    def block(body, args, name):
        return call(body, (tokens, width), args + params, name, flops)

    guess_z = from_odd(guess[0])
    guess_pair = from_pair(guess[0])
    first = block(choose_kernel, (guess_pair, guess_z, start_state), "first")
    first_z = from_odd(first)
    first_pair = from_pair(first)
    second_odd = block(odd_kernel, (first_pair,), "second_odd")
    second_z = from_odd(second_odd)
    second = block(even_kernel, (second_odd, first_z, start_state), "second")
    second_pair = from_pair(second)
    third = block(choose_kernel, (second_pair, second_z, start_state), "third")
    third_pair = from_pair(third)

    rows = tokens * width // LANES // places // cores
    part = call(part_kernel, (places, rows, LANES), (third_pair, second_pair), "part")
    parts = lax.all_to_all(part, "z", 0, 0, tiled=True)
    third, parts = lax.optimization_barrier((third, parts))
    third_z = from_odd(third)
    own = call(
        functools.partial(own_kernel, places * cores),
        (groups, rows + 8, LANES),
        (parts, coarse_gain),
        "own",
    )
    heard = lax.all_to_all(own, "outer", 0, 0, tiled=True)
    both = call(scan_kernel, (places, 2 * rows, LANES), (heard,), "scan", after=(third_z,))
    both = from_pair(lax.all_to_all(both, "z", 0, 0, tiled=True))
    return call(
        last_kernel,
        (1, tokens, width),
        (both, third_pair, third_z, start_state) + params,
        "last",
        flops,
    )


def solution(mesh):
    groups, inner = mesh.devices.shape
    fine = Mesh(mesh.devices.reshape(groups, inner // 2, 2), ALL)
    split = P(ALL, None, None)
    return jax.shard_map(
        per_device,
        mesh=fine,
        in_specs=(P(), split, split, split, P(ALL, None), P("outer", None)),
        out_specs=split,
        check_vma=False,
    )
```

```python
import functools

import jax
import jax.numpy as jnp
from jax import lax
from jax.experimental import pallas as pl
from jax.experimental.pallas import tpu as pltpu
from jax.sharding import Mesh, PartitionSpec as P

step_size = 0.5
ALL = ("outer", "z", "core")
LANES = 128


def from_odd(value):
    peers = lax.axis_size(ALL)
    return lax.ppermute(value, ALL, [(i, i + 1) for i in range(1, peers - 1, 2)])


def from_pair(value):
    return lax.all_gather(value, "core", axis=0)


def gelu(value):
    root = 0.7978845608028654
    inner = value * (root + (root * 0.044715) * (value * value))
    half = 0.5 * value
    return half + half * jnp.tanh(inner)


def layers(state, weight_in, weight_out, norm_gain):
    for level in range(weight_in.shape[0]):
        meansq = jnp.mean(state * state, axis=-1, keepdims=True)
        normed = (state * lax.rsqrt(meansq + 1e-06) * norm_gain[level : level + 1, :]).astype(
            jnp.bfloat16
        )
        hidden = jnp.dot(normed, weight_in[level], preferred_element_type=jnp.float32)
        hidden = gelu(hidden).astype(jnp.bfloat16)
        state = state + step_size * jnp.dot(
            hidden, weight_out[level], preferred_element_type=jnp.float32
        )
    return state


def call(body, out_shape, args, name, flops=0, after=()):
    count = len(args)

    def with_after(*refs):
        body(*refs[:count], refs[-1])

    return pl.pallas_call(
        with_after,
        out_shape=jax.ShapeDtypeStruct(out_shape, jnp.float32),
        in_specs=[pl.BlockSpec(memory_space=pltpu.VMEM)] * count
        + [pl.BlockSpec(memory_space=pl.ANY)] * len(after),
        out_specs=pl.BlockSpec(memory_space=pltpu.VMEM),
        compiler_params=pltpu.CompilerParams(vmem_limit_bytes=16 << 20),
        cost_estimate=pl.CostEstimate(
            flops=flops, bytes_accessed=sum(a.size * 4 for a in args), transcendentals=0
        ),
        name=name,
    )(*args, *after)


def load_kernel(*refs):
    count = len(refs) // 3
    copies = [
        pltpu.make_async_copy(refs[at], refs[count + at], refs[2 * count + at])
        for at in range(count)
    ]
    for copy in copies:
        copy.start()
    for copy in copies:
        copy.wait()


def loaded(args):
    return pl.pallas_call(
        load_kernel,
        out_shape=[pltpu.VMEM(a.shape, a.dtype) for a in args],
        in_specs=[pl.BlockSpec(memory_space=pl.ANY)] * len(args),
        out_specs=[pl.BlockSpec(memory_space=pltpu.VMEM)] * len(args),
        scratch_shapes=[pltpu.SemaphoreType.DMA(())] * len(args),
        compiler_params=pltpu.CompilerParams(vmem_limit_bytes=16 << 20),
        cost_estimate=pl.CostEstimate(
            flops=0,
            bytes_accessed=sum(a.size * a.dtype.itemsize for a in args),
            transcendentals=0,
        ),
        name="load",
    )(*[pltpu.with_memory_space_constraint(a, pltpu.HBM) for a in args])


def is_odd():
    return lax.axis_index("core") == 1


def is_first():
    return lax.axis_index(ALL) == 0


def odd_kernel(pair, weight_in, weight_out, norm_gain, out):
    @pl.when(is_odd())
    def _():
        out[...] = layers(pair[0], weight_in, weight_out, norm_gain)


def even_kernel(odd, hop, start, weight_in, weight_out, norm_gain, out):
    @pl.when(is_odd())
    def _():
        out[...] = odd[...]

    @pl.when(jnp.logical_not(is_odd()))
    def _():
        state = jnp.where(is_first(), start[...], hop[...])
        out[...] = layers(state, weight_in, weight_out, norm_gain)


def part_kernel(third, second, out):
    places, rows, lanes = out.shape
    tokens, width = third.shape[1:]
    half = width // 2
    across = half // lanes

    def piece(ref, which, at, right):
        down = pl.ds(at // across * rows, rows)
        side = pl.ds(right * half + at % across * lanes, lanes)
        return ref[which, down, side]

    for at in range(places):
        sums = []
        for right in range(2):
            sums.append(
                (piece(third, 0, at, right) - piece(second, 0, at, right))
                + (piece(third, 1, at, right) - piece(second, 1, at, right))
            )
        out[at] = jnp.where(is_odd(), sums[1], sums[0])


def gain_piece(gain, lanes):
    pieces = gain.shape[1] // lanes
    across = pieces // 2
    place = lax.axis_index("core") * across + lax.rem(lax.axis_index("z"), across)
    value = gain[:, 0:lanes]
    for at in range(1, pieces):
        value = jnp.where(place == at, gain[:, at * lanes : (at + 1) * lanes], value)
    return value


def own_kernel(count, parts, gain, out):
    places, rows, lanes = parts.shape
    own = parts[0]
    for at in range(1, places):
        own = own + parts[at]
    own = own / count
    spare = out.shape[1] - rows
    tail = jnp.broadcast_to(gain_piece(gain, lanes), (spare, lanes))
    for group in range(out.shape[0]):
        out[group, 0:rows, :] = own
        out[group, rows:, :] = tail


def scan_kernel(heard, out):
    groups = heard.shape[0]
    rows, lanes = out.shape[1] // 2, out.shape[2]
    group = lax.axis_index("outer")
    running = jnp.zeros((rows, lanes), jnp.float32)
    earlier, current = running, running
    for index in range(groups):
        earlier = jnp.where(index == group, running, earlier)
        running = heard[index, rows : rows + 1, :] * running + heard[index, 0:rows, :]
        current = jnp.where(index == group, running, current)
    for place in range(out.shape[0]):
        out[place, 0:rows, :] = earlier
        out[place, rows:, :] = current


def last_kernel(both, pair, hop, start, weight_in, weight_out, norm_gain, out):
    cores, places = both.shape[:2]
    rows, lanes = both.shape[2] // 2, both.shape[3]
    count = places * cores
    place = lax.axis_index("z") * cores + lax.axis_index("core")
    weight = place.astype(jnp.float32) / count
    across = hop.shape[1] // lanes // cores
    columns = []
    for core in range(cores):
        for side in range(across):
            pieces = []
            for down in range(places // across):
                at = down * across + side
                earlier, current = both[core, at, 0:rows, :], both[core, at, rows:, :]
                pieces.append(weight * current + (1.0 - weight) * earlier)
            columns.append(jnp.concatenate(pieces, axis=0))
    moved = jnp.where(is_odd(), pair[0], hop[...])
    state = moved + jnp.concatenate(columns, axis=1)
    state = jnp.where(is_first(), start[...], state)
    out[0] = layers(state, weight_in, weight_out, norm_gain)


def per_device(start_state, guess, weight_in, weight_out, norm_gain, coarse_gain):
    tokens, width = start_state.shape
    places, groups = lax.axis_size("z"), lax.axis_size("outer")
    cores = lax.axis_size("core")
    *params, start_state, coarse_gain = loaded(
        (weight_in, weight_out, norm_gain, start_state, coarse_gain)
    )
    params = tuple(params)
    flops = 4 * tokens * weight_in.size

    def block(body, args, name):
        return call(body, (tokens, width), args + params, name, flops)

    pairs = [from_pair(guess[0])]
    hop = from_odd(guess[0])
    for _ in range(3):
        odd = block(odd_kernel, (pairs[-1],), "odd")
        next_hop = from_odd(odd)
        state = block(even_kernel, (odd, hop, start_state), "even")
        pairs.append(from_pair(state))
        hop = next_hop
    second_pair, third_pair = pairs[2:]

    rows = tokens * width // LANES // places // cores
    part = call(part_kernel, (places, rows, LANES), (third_pair, second_pair), "part")
    parts, hop = lax.optimization_barrier((lax.all_to_all(part, "z", 0, 0, tiled=True), hop))
    own = call(
        functools.partial(own_kernel, places * cores),
        (groups, rows + 8, LANES),
        (parts, coarse_gain),
        "own",
    )
    heard = lax.all_to_all(own, "outer", 0, 0, tiled=True)
    both = call(scan_kernel, (places, 2 * rows, LANES), (heard,), "scan")
    both = from_pair(lax.all_to_all(both, "z", 0, 0, tiled=True))
    return call(
        last_kernel,
        (1, tokens, width),
        (both, third_pair, hop, start_state) + params,
        "last",
        flops,
    )


def solution(mesh):
    groups, inner = mesh.devices.shape
    fine = Mesh(mesh.devices.reshape(groups, inner // 2, 2), ALL)
    split = P(ALL, None, None)
    return jax.shard_map(
        per_device,
        mesh=fine,
        in_specs=(P(), split, split, split, P(ALL, None), P("outer", None)),
        out_specs=split,
        check_vma=False,
    )
```

```python
import functools

import jax
import jax.numpy as jnp
from jax import lax
from jax.experimental import pallas as pl
from jax.experimental.pallas import tpu as pltpu
from jax.sharding import Mesh, PartitionSpec as P

step_size = 0.5
ALL = ("outer", "z", "core")
LANES = 128


def from_odd(value):
    peers = lax.axis_size(ALL)
    return lax.ppermute(value, ALL, [(i, i + 1) for i in range(1, peers - 1, 2)])


def from_pair(value):
    return lax.all_gather(value, "core", axis=0)


def gelu(value):
    root = 0.7978845608028654
    inner = value * (root + (root * 0.044715) * (value * value))
    half = 0.5 * value
    return half + half * jnp.tanh(inner)


def layers(state, weight_in, weight_out, norm_gain):
    for level in range(weight_in.shape[0]):
        meansq = jnp.mean(state * state, axis=-1, keepdims=True)
        normed = (state * lax.rsqrt(meansq + 1e-06) * norm_gain[level : level + 1, :]).astype(
            jnp.bfloat16
        )
        hidden = jnp.dot(normed, weight_in[level], preferred_element_type=jnp.float32)
        hidden = gelu(hidden).astype(jnp.bfloat16)
        state = state + step_size * jnp.dot(
            hidden, weight_out[level], preferred_element_type=jnp.float32
        )
    return state


def call(body, out_shape, args, name, flops=0, after=()):
    count = len(args)

    def with_after(*refs):
        body(*refs[:count], refs[-1])

    return pl.pallas_call(
        with_after,
        out_shape=jax.ShapeDtypeStruct(out_shape, jnp.float32),
        in_specs=[pl.BlockSpec(memory_space=pltpu.VMEM)] * count
        + [pl.BlockSpec(memory_space=pl.ANY)] * len(after),
        out_specs=pl.BlockSpec(memory_space=pltpu.VMEM),
        compiler_params=pltpu.CompilerParams(vmem_limit_bytes=16 << 20),
        cost_estimate=pl.CostEstimate(
            flops=flops, bytes_accessed=sum(a.size * 4 for a in args), transcendentals=0
        ),
        name=name,
    )(*args, *after)


def load_kernel(*refs):
    count = len(refs) // 3
    copies = [
        pltpu.make_async_copy(refs[at], refs[count + at], refs[2 * count + at])
        for at in range(count)
    ]
    for copy in copies:
        copy.start()
    for copy in copies:
        copy.wait()


def loaded(args):
    return pl.pallas_call(
        load_kernel,
        out_shape=[pltpu.VMEM(a.shape, a.dtype) for a in args],
        in_specs=[pl.BlockSpec(memory_space=pl.ANY)] * len(args),
        out_specs=[pl.BlockSpec(memory_space=pltpu.VMEM)] * len(args),
        scratch_shapes=[pltpu.SemaphoreType.DMA(())] * len(args),
        compiler_params=pltpu.CompilerParams(vmem_limit_bytes=16 << 20),
        cost_estimate=pl.CostEstimate(
            flops=0,
            bytes_accessed=sum(a.size * a.dtype.itemsize for a in args),
            transcendentals=0,
        ),
        name="load",
    )(*[pltpu.with_memory_space_constraint(a, pltpu.HBM) for a in args])


def is_odd():
    return lax.axis_index("core") == 1


def is_first():
    return lax.axis_index(ALL) == 0


def odd_kernel(pair, weight_in, weight_out, norm_gain, out):
    @pl.when(is_odd())
    def _():
        out[...] = layers(pair[0], weight_in, weight_out, norm_gain)


def even_kernel(odd, hop, start, weight_in, weight_out, norm_gain, out):
    @pl.when(is_odd())
    def _():
        out[...] = odd[...]

    @pl.when(jnp.logical_not(is_odd()))
    def _():
        state = jnp.where(is_first(), start[...], hop[...])
        out[...] = layers(state, weight_in, weight_out, norm_gain)


def part_kernel(third, second, out):
    places, rows, lanes = out.shape
    tokens, width = third.shape[1:]
    half = width // 2
    across = half // lanes

    def piece(ref, which, at, right):
        down = pl.ds(at // across * rows, rows)
        side = pl.ds(right * half + at % across * lanes, lanes)
        return ref[which, down, side]

    for at in range(places):
        sums = []
        for right in range(2):
            sums.append(
                (piece(third, 0, at, right) - piece(second, 0, at, right))
                + (piece(third, 1, at, right) - piece(second, 1, at, right))
            )
        out[at] = jnp.where(is_odd(), sums[1], sums[0])


def gain_piece(gain, lanes):
    pieces = gain.shape[1] // lanes
    across = pieces // 2
    place = lax.axis_index("core") * across + lax.rem(lax.axis_index("z"), across)
    value = gain[:, 0:lanes]
    for at in range(1, pieces):
        value = jnp.where(place == at, gain[:, at * lanes : (at + 1) * lanes], value)
    return value


def own_kernel(count, parts, gain, out):
    places, rows, lanes = parts.shape
    own = parts[0]
    for at in range(1, places):
        own = own + parts[at]
    own = own / count
    spare = out.shape[1] - rows
    tail = jnp.broadcast_to(gain_piece(gain, lanes), (spare, lanes))
    for group in range(out.shape[0]):
        out[group, 0:rows, :] = own
        out[group, rows:, :] = tail


def scan_kernel(heard, out):
    groups = heard.shape[0]
    rows, lanes = out.shape[1] // 2, out.shape[2]
    group = lax.axis_index("outer")
    running = jnp.zeros((rows, lanes), jnp.float32)
    earlier, current = running, running
    for index in range(groups):
        earlier = jnp.where(index == group, running, earlier)
        running = heard[index, rows : rows + 1, :] * running + heard[index, 0:rows, :]
        current = jnp.where(index == group, running, current)
    for place in range(out.shape[0]):
        out[place, 0:rows, :] = earlier
        out[place, rows:, :] = current


def last_kernel(both, pair, hop, start, weight_in, weight_out, norm_gain, out):
    cores, places = both.shape[:2]
    rows, lanes = both.shape[2] // 2, both.shape[3]
    count = places * cores
    place = lax.axis_index("z") * cores + lax.axis_index("core")
    weight = place.astype(jnp.float32) / count
    across = hop.shape[1] // lanes // cores
    columns = []
    for core in range(cores):
        for side in range(across):
            pieces = []
            for down in range(places // across):
                at = down * across + side
                earlier, current = both[core, at, 0:rows, :], both[core, at, rows:, :]
                pieces.append(weight * current + (1.0 - weight) * earlier)
            columns.append(jnp.concatenate(pieces, axis=0))
    moved = jnp.where(is_odd(), pair[0], hop[...])
    state = moved + jnp.concatenate(columns, axis=1)
    state = jnp.where(is_first(), start[...], state)
    out[0] = layers(state, weight_in, weight_out, norm_gain)


def per_device(start_state, guess, weight_in, weight_out, norm_gain, coarse_gain):
    tokens, width = start_state.shape
    places, groups = lax.axis_size("z"), lax.axis_size("outer")
    cores = lax.axis_size("core")
    *params, start_state, coarse_gain = loaded(
        (weight_in, weight_out, norm_gain, start_state, coarse_gain)
    )
    params = tuple(params)
    flops = 4 * tokens * weight_in.size

    def block(body, args, name):
        return call(body, (tokens, width), args + params, name, flops)

    pairs = [from_pair(guess[0])]
    hop = from_odd(guess[0])
    for _ in range(3):
        odd = block(odd_kernel, (pairs[-1],), "odd")
        next_hop = from_odd(odd)
        state = block(even_kernel, (odd, hop, start_state), "even")
        pairs.append(from_pair(state))
        hop = next_hop
    second_pair, third_pair = pairs[2:]

    rows = tokens * width // LANES // places // cores
    part = call(part_kernel, (places, rows, LANES), (third_pair, second_pair), "part")
    parts = lax.all_to_all(part, "z", 0, 0, tiled=True)
    own = call(
        functools.partial(own_kernel, places * cores),
        (groups, rows + 8, LANES),
        (parts, coarse_gain),
        "own",
    )
    heard, hop = lax.optimization_barrier((lax.all_to_all(own, "outer", 0, 0, tiled=True), hop))
    both = call(scan_kernel, (places, 2 * rows, LANES), (heard,), "scan")
    both = from_pair(lax.all_to_all(both, "z", 0, 0, tiled=True))
    return call(
        last_kernel,
        (1, tokens, width),
        (both, third_pair, hop, start_state) + params,
        "last",
        flops,
    )


def solution(mesh):
    groups, inner = mesh.devices.shape
    fine = Mesh(mesh.devices.reshape(groups, inner // 2, 2), ALL)
    split = P(ALL, None, None)
    return jax.shard_map(
        per_device,
        mesh=fine,
        in_specs=(P(), split, split, split, P(ALL, None), P("outer", None)),
        out_specs=split,
        check_vma=False,
    )
```

```python
import functools

import jax
import jax.numpy as jnp
from jax import lax
from jax.experimental import pallas as pl
from jax.experimental.pallas import tpu as pltpu
from jax.sharding import Mesh, PartitionSpec as P

step_size = 0.5
ALL = ("outer", "z", "core")
LANES = 128


def from_odd(value, by=1):
    peers = lax.axis_size(ALL)
    return lax.ppermute(value, ALL, [(i, i + by) for i in range(1, peers - by, 2)])


def from_pair(value):
    return lax.all_gather(value, "core", axis=0)


def gelu(value):
    root = 0.7978845608028654
    inner = value * (root + (root * 0.044715) * (value * value))
    half = 0.5 * value
    return half + half * jnp.tanh(inner)


def layers(state, weight_in, weight_out, norm_gain, arriving=None):
    for level in range(weight_in.shape[0]):
        meansq = jnp.mean(state * state, axis=-1, keepdims=True)
        normed = (state * lax.rsqrt(meansq + 1e-06) * norm_gain[level : level + 1, :]).astype(
            jnp.bfloat16
        )
        hidden = jnp.dot(normed, weight_in[level], preferred_element_type=jnp.float32)
        hidden = gelu(hidden).astype(jnp.bfloat16)
        if arriving:
            arriving[level].wait()
        state = state + step_size * jnp.dot(
            hidden, weight_out[level], preferred_element_type=jnp.float32
        )
    return state


def call(body, out_shape, args, name, flops=0, kind=None, far=(), scratch=()):
    far = tuple(pltpu.with_memory_space_constraint(a, pltpu.HBM) for a in far)
    return pl.pallas_call(
        body,
        out_shape=(kind or jax.ShapeDtypeStruct)(out_shape, jnp.float32),
        in_specs=[pl.BlockSpec(memory_space=pl.ANY)] * len(far)
        + [pl.BlockSpec(memory_space=pltpu.VMEM)] * len(args),
        out_specs=pl.BlockSpec(memory_space=pltpu.VMEM),
        scratch_shapes=scratch,
        compiler_params=pltpu.CompilerParams(vmem_limit_bytes=16 << 20),
        cost_estimate=pl.CostEstimate(
            flops=flops, bytes_accessed=sum(a.size * 4 for a in args), transcendentals=0
        ),
        name=name,
    )(*far, *args)


def load_kernel(*refs):
    count = len(refs) // 3
    copies = [
        pltpu.make_async_copy(refs[at], refs[count + at], refs[2 * count + at])
        for at in range(count)
    ]
    for copy in copies:
        copy.start()
    for copy in copies:
        copy.wait()


def loaded(args):
    return pl.pallas_call(
        load_kernel,
        out_shape=[pltpu.VMEM(a.shape, a.dtype) for a in args],
        in_specs=[pl.BlockSpec(memory_space=pl.ANY)] * len(args),
        out_specs=[pl.BlockSpec(memory_space=pltpu.VMEM)] * len(args),
        scratch_shapes=[pltpu.SemaphoreType.DMA(())] * len(args),
        compiler_params=pltpu.CompilerParams(vmem_limit_bytes=16 << 20),
        cost_estimate=pl.CostEstimate(
            flops=0,
            bytes_accessed=sum(a.size * a.dtype.itemsize for a in args),
            transcendentals=0,
        ),
        name="load",
    )(*[pltpu.with_memory_space_constraint(a, pltpu.HBM) for a in args])


def is_odd():
    return lax.axis_index("core") == 1


def is_first():
    return lax.axis_index(ALL) == 0


def odd_kernel(pair, weight_in, weight_out, norm_gain, out):
    @pl.when(is_odd())
    def _():
        out[...] = layers(pair[0], weight_in, weight_out, norm_gain)


def even_kernel(odd, hop, start, weight_in, weight_out, norm_gain, out):
    @pl.when(is_odd())
    def _():
        out[...] = odd[...]

    @pl.when(jnp.logical_not(is_odd()))
    def _():
        state = jnp.where(is_first(), start[...], hop[...])
        out[...] = layers(state, weight_in, weight_out, norm_gain)


def part_kernel(third, second, out):
    places, rows, lanes = out.shape
    tokens, width = third.shape[1:]
    half = width // 2
    across = half // lanes

    def piece(ref, which, at, right):
        down = pl.ds(at // across * rows, rows)
        side = pl.ds(right * half + at % across * lanes, lanes)
        return ref[which, down, side]

    for at in range(places):
        sums = []
        for right in range(2):
            sums.append(
                (piece(third, 0, at, right) - piece(second, 0, at, right))
                + (piece(third, 1, at, right) - piece(second, 1, at, right))
            )
        out[at] = jnp.where(is_odd(), sums[1], sums[0])


def gain_piece(gain, lanes):
    pieces = gain.shape[1] // lanes
    across = pieces // 2
    place = lax.axis_index("core") * across + lax.rem(lax.axis_index("z"), across)
    value = gain[:, 0:lanes]
    for at in range(1, pieces):
        value = jnp.where(place == at, gain[:, at * lanes : (at + 1) * lanes], value)
    return value


def own_kernel(count, parts, gain, out):
    places, rows, lanes = parts.shape
    own = parts[0]
    for at in range(1, places):
        own = own + parts[at]
    own = own / count
    spare = out.shape[1] - rows
    tail = jnp.broadcast_to(gain_piece(gain, lanes), (spare, lanes))
    for group in range(out.shape[0]):
        out[group, 0:rows, :] = own
        out[group, rows:, :] = tail


def scan_kernel(heard, out):
    groups = heard.shape[0]
    rows, lanes = out.shape[1] // 2, out.shape[2]
    group = lax.axis_index("outer")
    running = jnp.zeros((rows, lanes), jnp.float32)
    earlier, current = running, running
    for index in range(groups):
        earlier = jnp.where(index == group, running, earlier)
        running = heard[index, rows : rows + 1, :] * running + heard[index, 0:rows, :]
        current = jnp.where(index == group, running, current)
    for place in range(out.shape[0]):
        out[place, 0:rows, :] = earlier
        out[place, rows:, :] = current


def last_kernel(
    far_weight, far_hop, both, pair, start, weight_in, norm_gain, out, weight_out, hop, sem
):
    levels = weight_out.shape[0]
    copies = [pltpu.make_async_copy(far_hop.at[1], hop, sem.at[levels])]
    for level in range(levels):
        copies.append(
            pltpu.make_async_copy(far_weight.at[level], weight_out.at[level], sem.at[level])
        )
    for copy in copies:
        copy.start()
    cores, places = both.shape[:2]
    rows, lanes = both.shape[2] // 2, both.shape[3]
    count = places * cores
    place = lax.axis_index("z") * cores + lax.axis_index("core")
    weight = place.astype(jnp.float32) / count
    across = hop.shape[1] // lanes // cores
    columns = []
    for core in range(cores):
        for side in range(across):
            pieces = []
            for down in range(places // across):
                at = down * across + side
                earlier, current = both[core, at, 0:rows, :], both[core, at, rows:, :]
                pieces.append(weight * current + (1.0 - weight) * earlier)
            columns.append(jnp.concatenate(pieces, axis=0))
    copies[0].wait()
    moved = jnp.where(is_odd(), pair[0], hop[...])
    state = moved + jnp.concatenate(columns, axis=1)
    state = jnp.where(is_first(), start[...], state)
    out[0] = layers(state, weight_in, weight_out, norm_gain, copies[1:])


def per_device(start_state, guess, weight_in, weight_out, norm_gain, coarse_gain):
    tokens, width = start_state.shape
    places, groups = lax.axis_size("z"), lax.axis_size("outer")
    cores = lax.axis_size("core")
    *params, start_state, coarse_gain = loaded(
        (weight_in, weight_out, norm_gain, start_state, coarse_gain)
    )
    params = tuple(params)
    flops = 4 * tokens * weight_in.size

    def block(body, args, name):
        return call(body, (tokens, width), args + params, name, flops)

    pairs = [from_pair(guess[0])]
    hop = from_odd(guess[0])
    for by in (1, 1, 2):
        odd = block(odd_kernel, (pairs[-1],), "odd")
        next_hop = from_odd(odd, by)
        state = block(even_kernel, (odd, hop, start_state), "even")
        pairs.append(from_pair(state))
        hop = next_hop
    second_pair, third_pair = pairs[2:]

    rows = tokens * width // LANES // places // cores
    part = call(part_kernel, (places, rows, LANES), (third_pair, second_pair), "part", 0, pltpu.HBM)
    parts = lax.all_to_all(part, "z", 0, 0, tiled=True)
    own = call(
        functools.partial(own_kernel, places * cores),
        (groups, rows + 8, LANES),
        (parts, coarse_gain),
        "own",
    )
    heard, hop = lax.optimization_barrier((lax.all_to_all(own, "outer", 0, 0, tiled=True), hop))
    both = call(scan_kernel, (places, 2 * rows, LANES), (heard,), "scan", 0, pltpu.HBM)
    both = from_pair(lax.all_to_all(both, "z", 0, 0, tiled=True))
    hop = from_pair(hop)
    return call(
        last_kernel,
        (1, tokens, width),
        (both, third_pair, start_state, params[0], params[2]),
        "last",
        flops,
        far=(weight_out, hop),
        scratch=[
            pltpu.VMEM(weight_out.shape, weight_out.dtype),
            pltpu.VMEM((tokens, width), jnp.float32),
            pltpu.SemaphoreType.DMA((weight_out.shape[0] + 1,)),
        ],
    )


def solution(mesh):
    groups, inner = mesh.devices.shape
    fine = Mesh(mesh.devices.reshape(groups, inner // 2, 2), ALL)
    split = P(ALL, None, None)
    return jax.shard_map(
        per_device,
        mesh=fine,
        in_specs=(P(), split, split, split, P(ALL, None), P("outer", None)),
        out_specs=split,
        check_vma=False,
    )
```

```python
import functools

import jax
import jax.numpy as jnp
from jax import lax
from jax.experimental import pallas as pl
from jax.experimental.pallas import tpu as pltpu
from jax.sharding import Mesh, PartitionSpec as P

step_size = 0.5
ALL = ("outer", "far", "near", "core")
PLACES = ("far", "near")
LANES = 128


def from_odd(value):
    peers = lax.axis_size(ALL)
    return lax.ppermute(value, ALL, [(i, i + 1) for i in range(1, peers - 1, 2)])


def from_pair(value):
    return lax.all_gather(value, "core", axis=0)


def gelu(value):
    root = 0.7978845608028654
    inner = value * (root + (root * 0.044715) * (value * value))
    half = 0.5 * value
    return half + half * jnp.tanh(inner)


def layers(state, weight_in, weight_out, norm_gain, arriving=None):
    for level in range(weight_in.shape[0]):
        meansq = jnp.mean(state * state, axis=-1, keepdims=True)
        normed = (state * lax.rsqrt(meansq + 1e-06) * norm_gain[level : level + 1, :]).astype(
            jnp.bfloat16
        )
        hidden = jnp.dot(normed, weight_in[level], preferred_element_type=jnp.float32)
        hidden = gelu(hidden).astype(jnp.bfloat16)
        if arriving:
            arriving[level].wait()
        state = state + step_size * jnp.dot(
            hidden, weight_out[level], preferred_element_type=jnp.float32
        )
    return state


def call(
    body, out_shape, args, name, flops=0, kind=jax.ShapeDtypeStruct, far=(), scratch=()
):
    far = tuple(pltpu.with_memory_space_constraint(a, pltpu.HBM) for a in far)
    return pl.pallas_call(
        body,
        out_shape=kind(out_shape, jnp.float32),
        in_specs=[pl.BlockSpec(memory_space=pl.ANY)] * len(far)
        + [pl.BlockSpec(memory_space=pltpu.VMEM)] * len(args),
        out_specs=pl.BlockSpec(memory_space=pltpu.VMEM),
        scratch_shapes=scratch,
        compiler_params=pltpu.CompilerParams(vmem_limit_bytes=16 << 20),
        cost_estimate=pl.CostEstimate(
            flops=flops, bytes_accessed=sum(a.size * 4 for a in args), transcendentals=0
        ),
        name=name,
    )(*far, *args)


def load_kernel(*refs):
    count = len(refs) // 3
    copies = [
        pltpu.make_async_copy(refs[at], refs[count + at], refs[2 * count + at])
        for at in range(count)
    ]
    for copy in copies:
        copy.start()
    for copy in copies:
        copy.wait()


def loaded(args):
    return pl.pallas_call(
        load_kernel,
        out_shape=[pltpu.VMEM(a.shape, a.dtype) for a in args],
        in_specs=[pl.BlockSpec(memory_space=pl.ANY)] * len(args),
        out_specs=[pl.BlockSpec(memory_space=pltpu.VMEM)] * len(args),
        scratch_shapes=[pltpu.SemaphoreType.DMA(())] * len(args),
        compiler_params=pltpu.CompilerParams(vmem_limit_bytes=16 << 20),
        cost_estimate=pl.CostEstimate(
            flops=0,
            bytes_accessed=sum(a.size * a.dtype.itemsize for a in args),
            transcendentals=0,
        ),
        name="load",
    )(*[pltpu.with_memory_space_constraint(a, pltpu.HBM) for a in args])


def is_odd():
    return lax.axis_index("core") == 1


def is_first():
    return lax.axis_index(ALL) == 0


def odd_kernel(pair, weight_in, weight_out, norm_gain, out):
    @pl.when(is_odd())
    def _():
        out[...] = layers(pair[0], weight_in, weight_out, norm_gain)


def even_kernel(odd, hop, start, weight_in, weight_out, norm_gain, out):
    @pl.when(is_odd())
    def _():
        out[...] = odd[...]

    @pl.when(jnp.logical_not(is_odd()))
    def _():
        state = jnp.where(is_first(), start[...], hop[...])
        out[...] = layers(state, weight_in, weight_out, norm_gain)


def part_kernel(third, second, out):
    places, rows, lanes = out.shape
    tokens, width = third.shape[1:]
    half = width // 2
    across = half // lanes

    def piece(ref, which, at, right):
        down = pl.ds(at // across * rows, rows)
        side = pl.ds(right * half + at % across * lanes, lanes)
        return ref[which, down, side]

    for at in range(places):
        sums = []
        for right in range(2):
            sums.append(
                (piece(third, 0, at, right) - piece(second, 0, at, right))
                + (piece(third, 1, at, right) - piece(second, 1, at, right))
            )
        out[at] = jnp.where(is_odd(), sums[1], sums[0])


def gain_piece(gain, lanes):
    pieces = gain.shape[1] // lanes
    across = pieces // 2
    place = lax.axis_index("core") * across + lax.rem(lax.axis_index(PLACES), across)
    value = gain[:, 0:lanes]
    for at in range(1, pieces):
        value = jnp.where(place == at, gain[:, at * lanes : (at + 1) * lanes], value)
    return value


def own_kernel(count, parts, gain, out):
    places, rows, lanes = parts.shape
    own = parts[0]
    for at in range(1, places):
        own = own + parts[at]
    own = own / count
    spare = out.shape[1] - rows
    tail = jnp.broadcast_to(gain_piece(gain, lanes), (spare, lanes))
    for group in range(out.shape[0]):
        out[group, 0:rows, :] = own
        out[group, rows:, :] = tail


def scan_kernel(heard, out):
    groups = heard.shape[0]
    rows, lanes = out.shape[1] // 2, out.shape[2]
    group = lax.axis_index("outer")
    running = jnp.zeros((rows, lanes), jnp.float32)
    earlier, current = running, running
    for index in range(groups):
        earlier = jnp.where(index == group, running, earlier)
        running = heard[index, rows : rows + 1, :] * running + heard[index, 0:rows, :]
        current = jnp.where(index == group, running, current)
    for place in range(out.shape[0]):
        out[place, 0:rows, :] = earlier
        out[place, rows:, :] = current


def last_kernel(
    far_weight, both, pair, hop, start, weight_in, norm_gain, out, weight_out, arrived
):
    arriving = [
        pltpu.make_async_copy(far_weight.at[level], weight_out.at[level], arrived.at[level])
        for level in range(weight_out.shape[0])
    ]
    for copy in arriving:
        copy.start()
    cores = pair.shape[0]
    nears = both.shape[0] // cores
    places = nears * both.shape[1]
    rows, lanes = both.shape[2] // 2, both.shape[3]
    count = places * cores
    place = lax.axis_index(PLACES) * cores + lax.axis_index("core")
    weight = place.astype(jnp.float32) / count
    across = hop.shape[1] // lanes // cores
    columns = []
    for core in range(cores):
        for side in range(across):
            pieces = []
            for down in range(places // across):
                at = down * across + side
                device, far = at % nears * cores + core, at // nears
                earlier, current = both[device, far, 0:rows, :], both[device, far, rows:, :]
                pieces.append(weight * current + (1.0 - weight) * earlier)
            columns.append(jnp.concatenate(pieces, axis=0))
    moved = jnp.where(is_odd(), pair[0], hop[...])
    state = moved + jnp.concatenate(columns, axis=1)
    state = jnp.where(is_first(), start[...], state)
    out[0] = layers(state, weight_in, weight_out, norm_gain, arriving)


def per_device(start_state, guess, weight_in, weight_out, norm_gain, coarse_gain):
    tokens, width = start_state.shape
    places, groups = lax.axis_size(PLACES), lax.axis_size("outer")
    cores = lax.axis_size("core")
    *params, start_state, coarse_gain = loaded(
        (weight_in, weight_out, norm_gain, start_state, coarse_gain)
    )
    params = tuple(params)
    flops = 4 * tokens * weight_in.size

    def block(body, args, name):
        return call(body, (tokens, width), args + params, name, flops)

    pairs = [from_pair(guess[0])]
    hop = from_odd(guess[0])
    for _ in range(3):
        odd = block(odd_kernel, (pairs[-1],), "odd")
        next_hop = from_odd(odd)
        state = block(even_kernel, (odd, hop, start_state), "even")
        pairs.append(from_pair(state))
        hop = next_hop
    second_pair, third_pair = pairs[2:]

    rows = tokens * width // LANES // places // cores
    part = call(part_kernel, (places, rows, LANES), (third_pair, second_pair), "part", 0, pltpu.HBM)
    parts = lax.all_to_all(part, PLACES, 0, 0, tiled=True)
    own = call(
        functools.partial(own_kernel, places * cores),
        (groups, rows + 8, LANES),
        (parts, coarse_gain),
        "own",
        0,
        pltpu.HBM,
    )
    heard, hop = lax.optimization_barrier((lax.all_to_all(own, "outer", 0, 0, tiled=True), hop))
    copies = lax.axis_size("far")
    both = call(scan_kernel, (copies, 2 * rows, LANES), (heard,), "scan")
    both = lax.all_to_all(both, "far", 0, 0, tiled=True)
    both = lax.all_gather(both, ("near", "core"), axis=0)
    return call(
        last_kernel,
        (1, tokens, width),
        (both, third_pair, hop, start_state, params[0], params[2]),
        "last",
        flops,
        far=(weight_out,),
        scratch=[
            pltpu.VMEM(weight_out.shape, weight_out.dtype),
            pltpu.SemaphoreType.DMA((weight_out.shape[0],)),
        ],
    )


def solution(mesh):
    groups, inner = mesh.devices.shape
    fine = Mesh(mesh.devices.reshape(groups, inner // 4, 2, 2), ALL)
    split = P(ALL, None, None)
    return jax.shard_map(
        per_device,
        mesh=fine,
        in_specs=(P(), split, split, split, P(ALL, None), P("outer", None)),
        out_specs=split,
        check_vma=False,
    )
```

```python
import functools

import jax
import jax.numpy as jnp
from jax import lax
from jax.experimental import pallas as pl
from jax.experimental.pallas import tpu as pltpu
from jax.sharding import Mesh, PartitionSpec as P

step_size = 0.5
ALL = ("outer", "far", "near", "core")
PLACES = ("far", "near")
LANES = 128


def from_odd(value):
    peers = lax.axis_size(ALL)
    return lax.ppermute(value, ALL, [(i, i + 1) for i in range(1, peers - 1, 2)])


def from_pair(value):
    return lax.all_gather(value, "core", axis=0)


def gelu(value):
    root = 0.7978845608028654
    inner = value * (root + (root * 0.044715) * (value * value))
    half = 0.5 * value
    return half + half * jnp.tanh(inner)


def layers(state, weight_in, weight_out, norm_gain):
    for level in range(weight_in.shape[0]):
        meansq = jnp.mean(state * state, axis=-1, keepdims=True)
        normed = (state * lax.rsqrt(meansq + 1e-06) * norm_gain[level : level + 1, :]).astype(
            jnp.bfloat16
        )
        hidden = jnp.dot(normed, weight_in[level], preferred_element_type=jnp.float32)
        hidden = gelu(hidden).astype(jnp.bfloat16)
        state = state + step_size * jnp.dot(
            hidden, weight_out[level], preferred_element_type=jnp.float32
        )
    return state


def call(
    body, out_shape, args, name, flops=0, kind=jax.ShapeDtypeStruct, far=(), scratch=()
):
    far = tuple(pltpu.with_memory_space_constraint(a, pltpu.HBM) for a in far)
    return pl.pallas_call(
        body,
        out_shape=kind(out_shape, jnp.float32),
        in_specs=[pl.BlockSpec(memory_space=pl.ANY)] * len(far)
        + [pl.BlockSpec(memory_space=pltpu.VMEM)] * len(args),
        out_specs=pl.BlockSpec(memory_space=pltpu.VMEM),
        scratch_shapes=scratch,
        compiler_params=pltpu.CompilerParams(vmem_limit_bytes=16 << 20),
        cost_estimate=pl.CostEstimate(
            flops=flops, bytes_accessed=sum(a.size * 4 for a in args), transcendentals=0
        ),
        name=name,
    )(*far, *args)


def load_kernel(*refs):
    count = len(refs) // 3
    copies = [
        pltpu.make_async_copy(refs[at], refs[count + at], refs[2 * count + at])
        for at in range(count)
    ]
    for copy in copies:
        copy.start()
    for copy in copies:
        copy.wait()


def loaded(args):
    return pl.pallas_call(
        load_kernel,
        out_shape=[pltpu.VMEM(a.shape, a.dtype) for a in args],
        in_specs=[pl.BlockSpec(memory_space=pl.ANY)] * len(args),
        out_specs=[pl.BlockSpec(memory_space=pltpu.VMEM)] * len(args),
        scratch_shapes=[pltpu.SemaphoreType.DMA(())] * len(args),
        compiler_params=pltpu.CompilerParams(vmem_limit_bytes=16 << 20),
        cost_estimate=pl.CostEstimate(
            flops=0,
            bytes_accessed=sum(a.size * a.dtype.itemsize for a in args),
            transcendentals=0,
        ),
        name="load",
    )(*[pltpu.with_memory_space_constraint(a, pltpu.HBM) for a in args])


def is_odd():
    return lax.axis_index("core") == 1


def is_first():
    return lax.axis_index(ALL) == 0


def odd_kernel(pair, weight_in, weight_out, norm_gain, out):
    @pl.when(is_odd())
    def _():
        out[...] = layers(pair[0], weight_in, weight_out, norm_gain)


def even_kernel(odd, hop, start, weight_in, weight_out, norm_gain, out):
    @pl.when(is_odd())
    def _():
        out[...] = odd[...]

    @pl.when(jnp.logical_not(is_odd()))
    def _():
        state = jnp.where(is_first(), start[...], hop[...])
        out[...] = layers(state, weight_in, weight_out, norm_gain)


def part_kernel(third, second, out):
    places, rows, lanes = out.shape
    tokens, width = third.shape[1:]
    half = width // 2
    across = half // lanes

    def piece(ref, which, at, right):
        down = pl.ds(at // across * rows, rows)
        side = pl.ds(right * half + at % across * lanes, lanes)
        return ref[which, down, side]

    for at in range(places):
        sums = []
        for right in range(2):
            sums.append(
                (piece(third, 0, at, right) - piece(second, 0, at, right))
                + (piece(third, 1, at, right) - piece(second, 1, at, right))
            )
        out[at] = jnp.where(is_odd(), sums[1], sums[0])


def gain_piece(gain, lanes):
    pieces = gain.shape[1] // lanes
    across = pieces // 2
    place = lax.axis_index("core") * across + lax.rem(lax.axis_index(PLACES), across)
    value = gain[:, 0:lanes]
    for at in range(1, pieces):
        value = jnp.where(place == at, gain[:, at * lanes : (at + 1) * lanes], value)
    return value


def own_kernel(count, parts, gain, out):
    places, rows, lanes = parts.shape
    own = parts[0]
    for at in range(1, places):
        own = own + parts[at]
    own = own / count
    spare = out.shape[1] - rows
    tail = jnp.broadcast_to(gain_piece(gain, lanes), (spare, lanes))
    for group in range(out.shape[0]):
        out[group, 0:rows, :] = own
        out[group, rows:, :] = tail


def scan_kernel(heard, out):
    groups = heard.shape[0]
    rows, lanes = out.shape[1] // 2, out.shape[2]
    group = lax.axis_index("outer")
    running = jnp.zeros((rows, lanes), jnp.float32)
    earlier, current = running, running
    for index in range(groups):
        earlier = jnp.where(index == group, running, earlier)
        running = heard[index, rows : rows + 1, :] * running + heard[index, 0:rows, :]
        current = jnp.where(index == group, running, current)
    for place in range(out.shape[0]):
        out[place, 0:rows, :] = earlier
        out[place, rows:, :] = current


def last_kernel(
    far_hop, both, pair, start, weight_in, weight_out, norm_gain, out, hop, arrived
):
    arriving = pltpu.make_async_copy(far_hop, hop, arrived)
    arriving.start()
    cores, nears = both.shape[:2]
    places = nears * both.shape[2]
    rows, lanes = both.shape[3] // 2, both.shape[4]
    count = places * cores
    place = lax.axis_index(PLACES) * cores + lax.axis_index("core")
    weight = place.astype(jnp.float32) / count
    across = hop.shape[1] // lanes // cores
    columns = []
    for core in range(cores):
        for side in range(across):
            pieces = []
            for down in range(places // across):
                at = down * across + side
                near, far = at % nears, at // nears
                earlier, current = both[core, near, far, 0:rows, :], both[core, near, far, rows:, :]
                pieces.append(weight * current + (1.0 - weight) * earlier)
            columns.append(jnp.concatenate(pieces, axis=0))
    arriving.wait()
    moved = jnp.where(is_odd(), pair[0], hop[...])
    state = moved + jnp.concatenate(columns, axis=1)
    state = jnp.where(is_first(), start[...], state)
    out[0] = layers(state, weight_in, weight_out, norm_gain)


def per_device(start_state, guess, weight_in, weight_out, norm_gain, coarse_gain):
    tokens, width = start_state.shape
    places, groups = lax.axis_size(PLACES), lax.axis_size("outer")
    cores = lax.axis_size("core")
    *params, start_state, coarse_gain = loaded(
        (weight_in, weight_out, norm_gain, start_state, coarse_gain)
    )
    params = tuple(params)
    flops = 4 * tokens * weight_in.size

    def block(body, args, name):
        return call(body, (tokens, width), args + params, name, flops)

    pairs = [from_pair(guess[0])]
    hop = from_odd(guess[0])
    for _ in range(3):
        odd = block(odd_kernel, (pairs[-1],), "odd")
        next_hop = from_odd(odd)
        state = block(even_kernel, (odd, hop, start_state), "even")
        pairs.append(from_pair(state))
        hop = next_hop
    second_pair, third_pair = pairs[2:]

    rows = tokens * width // LANES // places // cores
    part = call(part_kernel, (places, rows, LANES), (third_pair, second_pair), "part", 0, pltpu.HBM)
    parts = lax.all_to_all(part, PLACES, 0, 0, tiled=True)
    own = call(
        functools.partial(own_kernel, places * cores),
        (groups, rows + 8, LANES),
        (parts, coarse_gain),
        "own",
        0,
        pltpu.HBM,
    )
    heard, hop = lax.optimization_barrier((lax.all_to_all(own, "outer", 0, 0, tiled=True), hop))
    copies = lax.axis_size("far")
    both = call(scan_kernel, (copies, 2 * rows, LANES), (heard,), "scan")
    both = lax.all_to_all(both, "far", 0, 0, tiled=True)
    both = lax.all_gather(lax.all_gather(both, "near", axis=0), "core", axis=0)
    return call(
        last_kernel,
        (1, tokens, width),
        (both, third_pair, start_state) + params,
        "last",
        flops,
        far=(hop,),
        scratch=[pltpu.VMEM(hop.shape, hop.dtype), pltpu.SemaphoreType.DMA(())],
    )


def solution(mesh):
    groups, inner = mesh.devices.shape
    fine = Mesh(mesh.devices.reshape(groups, inner // 4, 2, 2), ALL)
    split = P(ALL, None, None)
    return jax.shard_map(
        per_device,
        mesh=fine,
        in_specs=(P(), split, split, split, P(ALL, None), P("outer", None)),
        out_specs=split,
        check_vma=False,
    )
```

```python
import functools

import jax
import jax.numpy as jnp
from jax import lax
from jax.experimental import pallas as pl
from jax.experimental.pallas import tpu as pltpu
from jax.sharding import Mesh, PartitionSpec as P

step_size = 0.5
ALL = ("outer", "far", "near", "core")
PLACES = ("far", "near")
LANES = 128


def from_odd(value):
    peers = lax.axis_size(ALL)
    return lax.ppermute(value, ALL, [(i, i + 1) for i in range(1, peers - 1, 2)])


def from_pair(value):
    return lax.all_gather(value, "core", axis=0)


def gelu(value):
    root = 0.7978845608028654
    inner = value * (root + (root * 0.044715) * (value * value))
    half = 0.5 * value
    return half + half * jnp.tanh(inner)


def layers(state, weight_in, weight_out, norm_gain, arriving=None):
    for level in range(weight_in.shape[0]):
        meansq = jnp.mean(state * state, axis=-1, keepdims=True)
        normed = (state * lax.rsqrt(meansq + 1e-06) * norm_gain[level : level + 1, :]).astype(
            jnp.bfloat16
        )
        hidden = jnp.dot(normed, weight_in[level], preferred_element_type=jnp.float32)
        hidden = gelu(hidden).astype(jnp.bfloat16)
        if arriving:
            arriving[level].wait()
        state = state + step_size * jnp.dot(
            hidden, weight_out[level], preferred_element_type=jnp.float32
        )
    return state


def call(
    body, out_shape, args, name, flops=0, kind=jax.ShapeDtypeStruct, far=(), scratch=()
):
    far = tuple(pltpu.with_memory_space_constraint(a, pltpu.HBM) for a in far)
    return pl.pallas_call(
        body,
        out_shape=kind(out_shape, jnp.float32),
        in_specs=[pl.BlockSpec(memory_space=pl.ANY)] * len(far)
        + [pl.BlockSpec(memory_space=pltpu.VMEM)] * len(args),
        out_specs=pl.BlockSpec(memory_space=pltpu.VMEM),
        scratch_shapes=scratch,
        compiler_params=pltpu.CompilerParams(vmem_limit_bytes=16 << 20),
        cost_estimate=pl.CostEstimate(
            flops=flops, bytes_accessed=sum(a.size * 4 for a in args), transcendentals=0
        ),
        name=name,
    )(*far, *args)


def load_kernel(*refs):
    count = len(refs) // 3
    copies = [
        pltpu.make_async_copy(refs[at], refs[count + at], refs[2 * count + at])
        for at in range(count)
    ]
    for copy in copies:
        copy.start()
    for copy in copies:
        copy.wait()


def loaded(args):
    return pl.pallas_call(
        load_kernel,
        out_shape=[pltpu.VMEM(a.shape, a.dtype) for a in args],
        in_specs=[pl.BlockSpec(memory_space=pl.ANY)] * len(args),
        out_specs=[pl.BlockSpec(memory_space=pltpu.VMEM)] * len(args),
        scratch_shapes=[pltpu.SemaphoreType.DMA(())] * len(args),
        compiler_params=pltpu.CompilerParams(vmem_limit_bytes=16 << 20),
        cost_estimate=pl.CostEstimate(
            flops=0,
            bytes_accessed=sum(a.size * a.dtype.itemsize for a in args),
            transcendentals=0,
        ),
        name="load",
    )(*[pltpu.with_memory_space_constraint(a, pltpu.HBM) for a in args])


def is_odd():
    return lax.axis_index("core") == 1


def is_first():
    return lax.axis_index(ALL) == 0


def odd_kernel(pair, weight_in, weight_out, norm_gain, out):
    @pl.when(is_odd())
    def _():
        out[...] = layers(pair[0], weight_in, weight_out, norm_gain)


def even_kernel(odd, hop, start, weight_in, weight_out, norm_gain, out):
    @pl.when(is_odd())
    def _():
        out[...] = odd[...]

    @pl.when(jnp.logical_not(is_odd()))
    def _():
        state = jnp.where(is_first(), start[...], hop[...])
        out[...] = layers(state, weight_in, weight_out, norm_gain)


def part_kernel(third, second, out):
    places, rows, lanes = out.shape
    tokens, width = third.shape[1:]
    half = width // 2
    across = half // lanes

    def piece(ref, which, at, right):
        down = pl.ds(at // across * rows, rows)
        side = pl.ds(right * half + at % across * lanes, lanes)
        return ref[which, down, side]

    for at in range(places):
        sums = []
        for right in range(2):
            sums.append(
                (piece(third, 0, at, right) - piece(second, 0, at, right))
                + (piece(third, 1, at, right) - piece(second, 1, at, right))
            )
        out[at] = jnp.where(is_odd(), sums[1], sums[0])


def gain_piece(gain, lanes):
    pieces = gain.shape[1] // lanes
    across = pieces // 2
    place = lax.axis_index("core") * across + lax.rem(lax.axis_index(PLACES), across)
    value = gain[:, 0:lanes]
    for at in range(1, pieces):
        value = jnp.where(place == at, gain[:, at * lanes : (at + 1) * lanes], value)
    return value


def own_kernel(count, parts, gain, out):
    places, rows, lanes = parts.shape
    own = parts[0]
    for at in range(1, places):
        own = own + parts[at]
    own = own / count
    spare = out.shape[1] - rows
    tail = jnp.broadcast_to(gain_piece(gain, lanes), (spare, lanes))
    for group in range(out.shape[0]):
        out[group, 0:rows, :] = own
        out[group, rows:, :] = tail


def scan_kernel(heard, out):
    groups = heard.shape[0]
    rows, lanes = out.shape[1] // 2, out.shape[2]
    group = lax.axis_index("outer")
    running = jnp.zeros((rows, lanes), jnp.float32)
    earlier, current = running, running
    for index in range(groups):
        earlier = jnp.where(index == group, running, earlier)
        running = heard[index, rows : rows + 1, :] * running + heard[index, 0:rows, :]
        current = jnp.where(index == group, running, current)
    for place in range(out.shape[0]):
        out[place, 0:rows, :] = earlier
        out[place, rows:, :] = current


def last_kernel(both, pair, hop, start, weight_in, weight_out, norm_gain, out):
    cores = pair.shape[0]
    nears = both.shape[0] // cores
    places = nears * both.shape[1]
    rows, lanes = both.shape[2] // 2, both.shape[3]
    count = places * cores
    place = lax.axis_index(PLACES) * cores + lax.axis_index("core")
    weight = place.astype(jnp.float32) / count
    across = hop.shape[1] // lanes // cores
    columns = []
    for core in range(cores):
        for side in range(across):
            pieces = []
            for down in range(places // across):
                at = down * across + side
                device, far = at % nears * cores + core, at // nears
                earlier, current = both[device, far, 0:rows, :], both[device, far, rows:, :]
                pieces.append(weight * current + (1.0 - weight) * earlier)
            columns.append(jnp.concatenate(pieces, axis=0))
    moved = jnp.where(is_odd(), pair[0], hop[...])
    state = moved + jnp.concatenate(columns, axis=1)
    state = jnp.where(is_first(), start[...], state)
    out[0] = layers(state, weight_in, weight_out, norm_gain)


def per_device(start_state, guess, weight_in, weight_out, norm_gain, coarse_gain):
    tokens, width = start_state.shape
    places, groups = lax.axis_size(PLACES), lax.axis_size("outer")
    cores = lax.axis_size("core")
    *params, start_state, coarse_gain = loaded(
        (weight_in, weight_out, norm_gain, start_state, coarse_gain)
    )
    params = tuple(params)
    flops = 4 * tokens * weight_in.size

    def block(body, args, name):
        return call(body, (tokens, width), args + params, name, flops)

    pairs = [from_pair(guess[0])]
    hop = from_odd(guess[0])
    for _ in range(3):
        odd = block(odd_kernel, (pairs[-1],), "odd")
        next_hop = from_odd(odd)
        state = block(even_kernel, (odd, hop, start_state), "even")
        pairs.append(from_pair(state))
        hop = next_hop
    second_pair, third_pair = pairs[2:]

    rows = tokens * width // LANES // places // cores
    part = call(part_kernel, (places, rows, LANES), (third_pair, second_pair), "part", 0, pltpu.HBM)
    parts = lax.all_to_all(part, PLACES, 0, 0, tiled=True)
    own = call(
        functools.partial(own_kernel, places * cores),
        (groups, rows + 8, LANES),
        (parts, coarse_gain),
        "own",
        0,
        pltpu.HBM,
    )
    heard, hop = lax.optimization_barrier((lax.all_to_all(own, "outer", 0, 0, tiled=True), hop))
    copies = lax.axis_size("far")
    both = call(scan_kernel, (copies, 2 * rows, LANES), (heard,), "scan", 12 * flops)
    both = lax.all_to_all(both, "far", 0, 0, tiled=True)
    both = lax.all_gather(both, ("near", "core"), axis=0)
    return call(
        last_kernel,
        (1, tokens, width),
        (both, third_pair, hop, start_state) + params,
        "last",
        flops,
    )


def solution(mesh):
    groups, inner = mesh.devices.shape
    fine = Mesh(mesh.devices.reshape(groups, inner // 4, 2, 2), ALL)
    split = P(ALL, None, None)
    return jax.shard_map(
        per_device,
        mesh=fine,
        in_specs=(P(), split, split, split, P(ALL, None), P("outer", None)),
        out_specs=split,
        check_vma=False,
    )
```

```python
import functools

import jax
import jax.numpy as jnp
from jax import lax
from jax.experimental import pallas as pl
from jax.experimental.pallas import tpu as pltpu
from jax.sharding import Mesh, PartitionSpec as P

step_size = 0.5
ALL = ("outer", "far", "near", "core")
PLACES = ("far", "near")
LANES = 128


def from_odd(value):
    peers = lax.axis_size(ALL)
    return lax.ppermute(value, ALL, [(i, i + 1) for i in range(1, peers - 1, 2)])


def from_pair(value):
    return lax.all_gather(value, "core", axis=0)


def gelu(value):
    root = 0.7978845608028654
    inner = value * (root + (root * 0.044715) * (value * value))
    half = 0.5 * value
    return half + half * jnp.tanh(inner)


def layers(state, weight_in, weight_out, norm_gain, arriving=None):
    for level in range(weight_in.shape[0]):
        meansq = jnp.mean(state * state, axis=-1, keepdims=True)
        normed = (state * lax.rsqrt(meansq + 1e-06) * norm_gain[level : level + 1, :]).astype(
            jnp.bfloat16
        )
        hidden = jnp.dot(normed, weight_in[level], preferred_element_type=jnp.float32)
        hidden = gelu(hidden).astype(jnp.bfloat16)
        if arriving:
            arriving[level].wait()
        state = state + step_size * jnp.dot(
            hidden, weight_out[level], preferred_element_type=jnp.float32
        )
    return state


def call(
    body, out_shape, args, name, flops=0, kind=jax.ShapeDtypeStruct, far=(), scratch=()
):
    far = tuple(pltpu.with_memory_space_constraint(a, pltpu.HBM) for a in far)
    return pl.pallas_call(
        body,
        out_shape=kind(out_shape, jnp.float32),
        in_specs=[pl.BlockSpec(memory_space=pl.ANY)] * len(far)
        + [pl.BlockSpec(memory_space=pltpu.VMEM)] * len(args),
        out_specs=pl.BlockSpec(memory_space=pltpu.VMEM),
        scratch_shapes=scratch,
        compiler_params=pltpu.CompilerParams(vmem_limit_bytes=16 << 20),
        cost_estimate=pl.CostEstimate(
            flops=flops, bytes_accessed=sum(a.size * 4 for a in args), transcendentals=0
        ),
        name=name,
    )(*far, *args)


def load_kernel(*refs):
    count = len(refs) // 3
    copies = [
        pltpu.make_async_copy(refs[at], refs[count + at], refs[2 * count + at])
        for at in range(count)
    ]
    for copy in copies:
        copy.start()
    for copy in copies:
        copy.wait()


def loaded(args):
    return pl.pallas_call(
        load_kernel,
        out_shape=[pltpu.VMEM(a.shape, a.dtype) for a in args],
        in_specs=[pl.BlockSpec(memory_space=pl.ANY)] * len(args),
        out_specs=[pl.BlockSpec(memory_space=pltpu.VMEM)] * len(args),
        scratch_shapes=[pltpu.SemaphoreType.DMA(())] * len(args),
        compiler_params=pltpu.CompilerParams(vmem_limit_bytes=16 << 20),
        cost_estimate=pl.CostEstimate(
            flops=0,
            bytes_accessed=sum(a.size * a.dtype.itemsize for a in args),
            transcendentals=0,
        ),
        name="load",
    )(*[pltpu.with_memory_space_constraint(a, pltpu.HBM) for a in args])


def is_odd():
    return lax.axis_index("core") == 1


def is_first():
    return lax.axis_index(ALL) == 0


def odd_kernel(pair, weight_in, weight_out, norm_gain, out):
    @pl.when(is_odd())
    def _():
        out[...] = layers(pair[0], weight_in, weight_out, norm_gain)


def even_kernel(odd, hop, start, weight_in, weight_out, norm_gain, out):
    @pl.when(is_odd())
    def _():
        out[...] = odd[...]

    @pl.when(jnp.logical_not(is_odd()))
    def _():
        state = jnp.where(is_first(), start[...], hop[...])
        out[...] = layers(state, weight_in, weight_out, norm_gain)


def part_kernel(third, second, out):
    places, rows, lanes = out.shape
    tokens, width = third.shape[1:]
    half = width // 2
    across = half // lanes

    def piece(ref, which, at, right):
        down = pl.ds(at // across * rows, rows)
        side = pl.ds(right * half + at % across * lanes, lanes)
        return ref[which, down, side]

    for at in range(places):
        sums = []
        for right in range(2):
            sums.append(
                (piece(third, 0, at, right) - piece(second, 0, at, right))
                + (piece(third, 1, at, right) - piece(second, 1, at, right))
            )
        out[at] = jnp.where(is_odd(), sums[1], sums[0])


def gain_piece(gain, lanes):
    pieces = gain.shape[1] // lanes
    across = pieces // 2
    place = lax.axis_index("core") * across + lax.rem(lax.axis_index(PLACES), across)
    value = gain[:, 0:lanes]
    for at in range(1, pieces):
        value = jnp.where(place == at, gain[:, at * lanes : (at + 1) * lanes], value)
    return value


def moved_kernel(pair, hop, out):
    out[...] = jnp.where(is_odd(), pair[0], hop[...])


def own_kernel(count, parts, gain, out):
    places, rows, lanes = parts.shape
    own = parts[0]
    for at in range(1, places):
        own = own + parts[at]
    own = own / count
    spare = out.shape[1] - rows
    tail = jnp.broadcast_to(gain_piece(gain, lanes), (spare, lanes))
    for group in range(out.shape[0]):
        out[group, 0:rows, :] = own
        out[group, rows:, :] = tail


def scan_kernel(heard, out):
    groups = heard.shape[0]
    rows, lanes = out.shape[1] // 2, out.shape[2]
    group = lax.axis_index("outer")
    running = jnp.zeros((rows, lanes), jnp.float32)
    earlier, current = running, running
    for index in range(groups):
        earlier = jnp.where(index == group, running, earlier)
        running = heard[index, rows : rows + 1, :] * running + heard[index, 0:rows, :]
        current = jnp.where(index == group, running, current)
    for place in range(out.shape[0]):
        out[place, 0:rows, :] = earlier
        out[place, rows:, :] = current


def last_kernel(both, moved, start, weight_in, weight_out, norm_gain, out):
    cores = 2
    nears = both.shape[0] // cores
    places = nears * both.shape[1]
    rows, lanes = both.shape[2] // 2, both.shape[3]
    count = places * cores
    place = lax.axis_index(PLACES) * cores + lax.axis_index("core")
    weight = place.astype(jnp.float32) / count
    across = moved.shape[1] // lanes // cores
    columns = []
    for core in range(cores):
        for side in range(across):
            pieces = []
            for down in range(places // across):
                at = down * across + side
                device, far = at % nears * cores + core, at // nears
                earlier, current = both[device, far, 0:rows, :], both[device, far, rows:, :]
                pieces.append(weight * current + (1.0 - weight) * earlier)
            columns.append(jnp.concatenate(pieces, axis=0))
    state = moved[...] + jnp.concatenate(columns, axis=1)
    state = jnp.where(is_first(), start[...], state)
    out[0] = layers(state, weight_in, weight_out, norm_gain)


def per_device(start_state, guess, weight_in, weight_out, norm_gain, coarse_gain):
    tokens, width = start_state.shape
    places, groups = lax.axis_size(PLACES), lax.axis_size("outer")
    cores = lax.axis_size("core")
    *params, start_state, coarse_gain = loaded(
        (weight_in, weight_out, norm_gain, start_state, coarse_gain)
    )
    params = tuple(params)
    flops = 4 * tokens * weight_in.size

    def block(body, args, name):
        return call(body, (tokens, width), args + params, name, flops)

    pairs = [from_pair(guess[0])]
    hop = from_odd(guess[0])
    for _ in range(3):
        odd = block(odd_kernel, (pairs[-1],), "odd")
        next_hop = from_odd(odd)
        state = block(even_kernel, (odd, hop, start_state), "even")
        pairs.append(from_pair(state))
        hop = next_hop
    second_pair, third_pair = pairs[2:]

    rows = tokens * width // LANES // places // cores
    part = call(part_kernel, (places, rows, LANES), (third_pair, second_pair), "part", 0, pltpu.HBM)
    parts = lax.all_to_all(part, PLACES, 0, 0, tiled=True)
    own = call(
        functools.partial(own_kernel, places * cores),
        (groups, rows + 8, LANES),
        (parts, coarse_gain),
        "own",
        0,
        pltpu.HBM,
    )
    moved = call(moved_kernel, (tokens, width), (third_pair, hop), "moved")
    heard = lax.all_to_all(own, "outer", 0, 0, tiled=True)
    heard, moved = lax.optimization_barrier((heard, moved))
    copies = lax.axis_size("far")
    both = call(scan_kernel, (copies, 2 * rows, LANES), (heard,), "scan", 12 * flops)
    both = lax.all_to_all(both, "far", 0, 0, tiled=True)
    both = lax.all_gather(both, ("near", "core"), axis=0)
    return call(
        last_kernel,
        (1, tokens, width),
        (both, moved, start_state) + params,
        "last",
        flops,
    )


def solution(mesh):
    groups, inner = mesh.devices.shape
    fine = Mesh(mesh.devices.reshape(groups, inner // 4, 2, 2), ALL)
    split = P(ALL, None, None)
    return jax.shard_map(
        per_device,
        mesh=fine,
        in_specs=(P(), split, split, split, P(ALL, None), P("outer", None)),
        out_specs=split,
        check_vma=False,
    )
```

```python
import functools

import jax
import jax.numpy as jnp
from jax import lax
from jax.experimental import pallas as pl
from jax.experimental.pallas import tpu as pltpu
from jax.sharding import Mesh, PartitionSpec as P

step_size = 0.5
ALL = ("outer", "far", "near", "core")
PLACES = ("far", "near")
LANES = 128


def from_odd(value):
    peers = lax.axis_size(ALL)
    return lax.ppermute(value, ALL, [(i, i + 1) for i in range(1, peers - 1, 2)])


def from_pair(value):
    return lax.all_gather(value, "core", axis=0)


def gelu(value):
    root = 0.7978845608028654
    inner = value * (root + (root * 0.044715) * (value * value))
    half = 0.5 * value
    return half + half * jnp.tanh(inner)


def layers(state, weight_in, weight_out, norm_gain, arriving=None):
    for level in range(weight_in.shape[0]):
        meansq = jnp.mean(state * state, axis=-1, keepdims=True)
        normed = (state * lax.rsqrt(meansq + 1e-06) * norm_gain[level : level + 1, :]).astype(
            jnp.bfloat16
        )
        hidden = jnp.dot(normed, weight_in[level], preferred_element_type=jnp.float32)
        hidden = gelu(hidden).astype(jnp.bfloat16)
        if arriving:
            arriving[level].wait()
        state = state + step_size * jnp.dot(
            hidden, weight_out[level], preferred_element_type=jnp.float32
        )
    return state


def call(
    body, out_shape, args, name, flops=0, kind=jax.ShapeDtypeStruct, far=(), scratch=()
):
    far = tuple(pltpu.with_memory_space_constraint(a, pltpu.HBM) for a in far)
    return pl.pallas_call(
        body,
        out_shape=kind(out_shape, jnp.float32),
        in_specs=[pl.BlockSpec(memory_space=pl.ANY)] * len(far)
        + [pl.BlockSpec(memory_space=pltpu.VMEM)] * len(args),
        out_specs=pl.BlockSpec(memory_space=pltpu.VMEM),
        scratch_shapes=scratch,
        compiler_params=pltpu.CompilerParams(vmem_limit_bytes=16 << 20),
        cost_estimate=pl.CostEstimate(
            flops=flops, bytes_accessed=sum(a.size * 4 for a in args), transcendentals=0
        ),
        name=name,
    )(*far, *args)


def load_kernel(*refs):
    count = len(refs) // 3
    copies = [
        pltpu.make_async_copy(refs[at], refs[count + at], refs[2 * count + at])
        for at in range(count)
    ]
    for copy in copies:
        copy.start()
    for copy in copies:
        copy.wait()


def loaded(args):
    return pl.pallas_call(
        load_kernel,
        out_shape=[pltpu.VMEM(a.shape, a.dtype) for a in args],
        in_specs=[pl.BlockSpec(memory_space=pl.ANY)] * len(args),
        out_specs=[pl.BlockSpec(memory_space=pltpu.VMEM)] * len(args),
        scratch_shapes=[pltpu.SemaphoreType.DMA(())] * len(args),
        compiler_params=pltpu.CompilerParams(vmem_limit_bytes=16 << 20),
        cost_estimate=pl.CostEstimate(
            flops=0,
            bytes_accessed=sum(a.size * a.dtype.itemsize for a in args),
            transcendentals=0,
        ),
        name="load",
    )(*[pltpu.with_memory_space_constraint(a, pltpu.HBM) for a in args])


def is_odd():
    return lax.axis_index("core") == 1


def is_first():
    return lax.axis_index(ALL) == 0


def odd_kernel(pair, weight_in, weight_out, norm_gain, out):
    @pl.when(is_odd())
    def _():
        out[...] = layers(pair[0], weight_in, weight_out, norm_gain)


def even_kernel(odd, hop, start, weight_in, weight_out, norm_gain, out):
    @pl.when(is_odd())
    def _():
        out[...] = odd[...]

    @pl.when(jnp.logical_not(is_odd()))
    def _():
        state = jnp.where(is_first(), start[...], hop[...])
        out[...] = layers(state, weight_in, weight_out, norm_gain)


def part_kernel(third, second, out):
    places, rows, lanes = out.shape
    tokens, width = third.shape[1:]
    half = width // 2
    across = half // lanes

    def piece(ref, which, at, right):
        down = pl.ds(at // across * rows, rows)
        side = pl.ds(right * half + at % across * lanes, lanes)
        return ref[which, down, side]

    for at in range(places):
        sums = []
        for right in range(2):
            sums.append(
                (piece(third, 0, at, right) - piece(second, 0, at, right))
                + (piece(third, 1, at, right) - piece(second, 1, at, right))
            )
        out[at] = jnp.where(is_odd(), sums[1], sums[0])


def gain_piece(gain, lanes):
    pieces = gain.shape[1] // lanes
    across = pieces // 2
    place = lax.axis_index("core") * across + lax.rem(lax.axis_index(PLACES), across)
    value = gain[:, 0:lanes]
    for at in range(1, pieces):
        value = jnp.where(place == at, gain[:, at * lanes : (at + 1) * lanes], value)
    return value


def moved_kernel(pair, hop, start, out):
    even = jnp.where(is_first(), start[...], hop[...])
    out[...] = jnp.where(is_odd(), pair[0], even)


def own_kernel(count, parts, gain, out):
    places, rows, lanes = parts.shape
    own = parts[0]
    for at in range(1, places):
        own = own + parts[at]
    own = own / count
    spare = out.shape[1] - rows
    tail = jnp.broadcast_to(gain_piece(gain, lanes), (spare, lanes))
    for group in range(out.shape[0]):
        out[group, 0:rows, :] = own
        out[group, rows:, :] = tail


def scan_kernel(heard, out):
    groups = heard.shape[0]
    rows, lanes = out.shape[1] // 2, out.shape[2]
    group = lax.axis_index("outer")
    running = jnp.zeros((rows, lanes), jnp.float32)
    earlier, current = running, running
    for index in range(groups):
        earlier = jnp.where(index == group, running, earlier)
        running = heard[index, rows : rows + 1, :] * running + heard[index, 0:rows, :]
        current = jnp.where(index == group, running, current)
    for place in range(out.shape[0]):
        out[place, 0:rows, :] = earlier
        out[place, rows:, :] = current


def last_kernel(both, moved, weight_in, weight_out, norm_gain, out):
    cores = 2
    nears = both.shape[0] // cores
    places = nears * both.shape[1]
    rows, lanes = both.shape[2] // 2, both.shape[3]
    count = places * cores
    place = lax.axis_index(PLACES) * cores + lax.axis_index("core")
    weight = place.astype(jnp.float32) / count
    across = moved.shape[1] // lanes // cores
    columns = []
    for core in range(cores):
        for side in range(across):
            pieces = []
            for down in range(places // across):
                at = down * across + side
                device, far = at % nears * cores + core, at // nears
                earlier, current = both[device, far, 0:rows, :], both[device, far, rows:, :]
                pieces.append(weight * current + (1.0 - weight) * earlier)
            columns.append(jnp.concatenate(pieces, axis=0))
    state = moved[...] + jnp.concatenate(columns, axis=1)
    out[0] = layers(state, weight_in, weight_out, norm_gain)


def per_device(start_state, guess, weight_in, weight_out, norm_gain, coarse_gain):
    tokens, width = start_state.shape
    places, groups = lax.axis_size(PLACES), lax.axis_size("outer")
    cores = lax.axis_size("core")
    *params, start_state, coarse_gain = loaded(
        (weight_in, weight_out, norm_gain, start_state, coarse_gain)
    )
    params = tuple(params)
    flops = 4 * tokens * weight_in.size

    def block(body, args, name):
        return call(body, (tokens, width), args + params, name, flops)

    pairs = [from_pair(guess[0])]
    hop = from_odd(guess[0])
    for _ in range(3):
        odd = block(odd_kernel, (pairs[-1],), "odd")
        next_hop = from_odd(odd)
        state = block(even_kernel, (odd, hop, start_state), "even")
        pairs.append(from_pair(state))
        hop = next_hop
    second_pair, third_pair = pairs[2:]

    rows = tokens * width // LANES // places // cores
    part = call(part_kernel, (places, rows, LANES), (third_pair, second_pair), "part", 0, pltpu.HBM)
    parts = lax.all_to_all(part, PLACES, 0, 0, tiled=True)
    own = call(
        functools.partial(own_kernel, places * cores),
        (groups, rows + 8, LANES),
        (parts, coarse_gain),
        "own",
        0,
        pltpu.HBM,
    )
    moved = call(moved_kernel, (tokens, width), (third_pair, hop, start_state), "moved")
    heard = lax.all_to_all(own, "outer", 0, 0, tiled=True)
    heard, moved = lax.optimization_barrier((heard, moved))
    copies = lax.axis_size("far")
    both = call(scan_kernel, (copies, 2 * rows, LANES), (heard,), "scan", 12 * flops)
    both = lax.all_to_all(both, "far", 0, 0, tiled=True)
    both = lax.all_gather(both, ("near", "core"), axis=0)
    return call(
        last_kernel,
        (1, tokens, width),
        (both, moved) + params,
        "last",
        flops,
    )


def solution(mesh):
    groups, inner = mesh.devices.shape
    fine = Mesh(mesh.devices.reshape(groups, inner // 4, 2, 2), ALL)
    split = P(ALL, None, None)
    return jax.shard_map(
        per_device,
        mesh=fine,
        in_specs=(P(), split, split, split, P(ALL, None), P("outer", None)),
        out_specs=split,
        check_vma=False,
    )
```
